32 devices in a mesh: tm: 4 (over y, x), row: 4 (over z), col: 2 (over core).
Axes of the slice: x: 2, y: 2, z: 4, core: 2. Of those that a mesh axis runs over, the one named last changes fastest.
Arguments:
- features: float32 [8, 32, 64, 128], P('tm', 'row', 'col'), may hold values from -100 to 100
- gain_first: float32 [128], replicated, may hold values from 0.1 to 1.9
- shift_first: float32 [128], replicated, may hold values from -3 to 3
- weight_first: float32 [3, 3, 3, 128, 128], replicated, may hold values from -0.109375 to 0.109375
- gain_second: float32 [128], replicated, may hold values from 0.1 to 1.9
- shift_second: float32 [128], replicated, may hold values from -3 to 3
- weight_second: float32 [3, 3, 3, 128, 128], replicated, may hold values from -0.109375 to 0.109375
- bias_second: float32 [128], replicated, may hold values from -3 to 3
Outputs:
- encoded: float32 [8, 32, 64, 128], P('tm', 'row', 'col')
The draws below stay inside these ranges and needn't reach their ends.
All inputs are finite; a program needn't handle non-finite values.
Results may differ from the reference program's by a relative error of at most 0.00005.
Values sent between devices are 32-bit elements; how exact they have to be, the bound alone decides.
A program may use at most 64 MiB of HBM per device.

```python
import math
import jax
import jax.numpy as jnp
from jax import lax

C = 128
GROUPS = 32
NT = 8
NH = 32
NW = 64


def draw_features(key, part):
    key = jax.random.fold_in(key, 11)
    key_base, key_cell, key_chan = jax.random.split(key, 3)
    shape = (NT, NH, NW, C)
    frame_pos = (jnp.arange(NT, dtype=jnp.float32) / NT).reshape(NT, 1, 1, 1)
    row_pos = (jnp.arange(NH, dtype=jnp.float32) / NH).reshape(1, NH, 1, 1)
    col_pos = (jnp.arange(NW, dtype=jnp.float32) / NW).reshape(1, 1, NW, 1)
    ramp = jnp.exp(math.log(3.0) * (row_pos + 0.5 * (frame_pos + col_pos) - 1.0))
    cell_scale = jnp.exp(math.log(10.0) * (jax.random.uniform(key_cell, (NT, NH, NW, 1), jnp.float32) - 0.5))
    chan_scale = jnp.exp(math.log(10.0) * (jax.random.uniform(key_chan, (1, 1, 1, C), jnp.float32) - 0.5))
    base = jnp.clip(jax.random.normal(key_base, shape, jnp.float32), -3.0, 3.0)
    return base * cell_scale * chan_scale * ramp


def bell_draw(own_key, extent, deviation, bound, kind=jnp.bfloat16):
    entries = jax.random.normal(own_key, extent, jnp.float32) * deviation
    return jnp.minimum(jnp.maximum(entries, -bound), bound).astype(kind)


def setup_inputs(seed: int = 0) -> dict:
    seeds = jax.random.split(jax.random.key(seed), 9)
    return {
        "features": draw_features(jax.random.fold_in(seeds[8], 71), 0),
        "gain_first": jnp.clip(1.0 + 0.18 * jax.random.normal(seeds[1], (C,), jnp.float32), 0.1, 1.9),
        "shift_first": bell_draw(seeds[2], (C,), 0.5, 3.0, jnp.float32),
        "weight_first": bell_draw(seeds[3], (3, 3, 3, C, C), (27 * C) ** -0.5, 0.109375, jnp.float32),
        "gain_second": jnp.clip(1.0 + 0.18 * jax.random.normal(seeds[4], (C,), jnp.float32), 0.1, 1.9),
        "shift_second": bell_draw(seeds[5], (C,), 0.5, 3.0, jnp.float32),
        "weight_second": bell_draw(seeds[6], (3, 3, 3, C, C), (27 * C) ** -0.5, 0.109375, jnp.float32),
        "bias_second": bell_draw(seeds[7], (C,), 0.5, 3.0, jnp.float32),
    }


epsilon = 1e-06

def norm_act(values, gain, offset):
    grouped = values.reshape(NT, NH, NW, GROUPS, C // GROUPS)
    average = lax.optimization_barrier(jnp.mean(grouped, axis=(0, 1, 2, 4), keepdims=True))
    spread = lax.optimization_barrier(jnp.mean(jnp.square(grouped - average), axis=(0, 1, 2, 4), keepdims=True))
    normed = ((grouped - average) * lax.rsqrt(spread + epsilon)).reshape(values.shape)
    return jax.nn.silu(normed * gain + offset)

def causal_conv(activated, weights):
    padded = jnp.concatenate([activated[:1], activated[:1], activated], axis=0)
    result = lax.conv_general_dilated(padded[None], weights, (1, 1, 1), ((0, 0), (1, 1), (1, 1)), dimension_numbers=('NDHWC', 'DHWIO', 'NDHWC'), precision=lax.Precision.HIGHEST)
    return result[0]

def reference(features, gain_first, shift_first, weight_first, gain_second, shift_second, weight_second, bias_second):
    hidden = causal_conv(norm_act(features, gain_first, shift_first), weight_first)
    second = norm_act(hidden, gain_second, shift_second)
    return features + causal_conv(second, weight_second) + bias_second
```

```python
import functools
import jax
import jax.numpy as jnp
from jax import lax
from jax.experimental import pallas as pl
from jax.experimental.pallas import tpu as pltpu
from jax.sharding import PartitionSpec as P

GROUPS = 32
MESH = pl.DeviceIdType.MESH
epsilon = 1e-06
F32 = jnp.float32
BF16 = jnp.bfloat16
STEPS = [
    (ahead, down, right)
    for ahead in (0, 1)
    for down in (-1, 0, 1)
    for right in (-1, 0, 1)
    if (ahead, down, right) != (0, 0, 0)
]


def repeat(count, body):
    if count <= 8:
        for i in range(count):
            body(i)
    else:
        lax.fori_loop(0, count, lambda i, _: (body(i), 0)[1], 0)


def group_total(value):
    channels = value.shape[-1]
    lane = lax.broadcasted_iota(jnp.int32, value.shape, 1)
    step = 1
    while step < channels // GROUPS:
        upper = pltpu.roll(value, channels - step, 1)
        lower = pltpu.roll(value, step, 1)
        value = value + jnp.where((lane & step) == 0, upper, lower)
        step *= 2
    return value


def split(value):
    high = value.astype(BF16)
    return high, (value - high.astype(F32)).astype(BF16)


def kernel(
    counts,
    feat_hbm, gain1, shift1, w1_hbm, gain2, shift2, w2_hbm, bias,
    out_ref,
    x_ref, hid_ref, w_raw, w_split, high, low, part,
    edge_cols, corners, front, got_rows, got_cols, got_corners, stat_a, stat_b,
    load_sem, halo_send, halo_recv, a_send, a_recv, b_send, b_recv,
):
    n_tm, n_row, n_col = counts
    n_rc = n_row * n_col
    tm, row, col = lax.axis_index("tm"), lax.axis_index("row"), lax.axis_index("col")
    rc = row * n_col + col
    frames, height, width, channels = x_ref.shape
    cells = frames * height * width
    per_group = channels // GROUPS
    taps = 9 * channels

    def exists(ahead, down, right):
        ok = (row + down >= 0) & (row + down < n_row)
        ok = ok & (col + right >= 0) & (col + right < n_col)
        return ok & (tm + ahead >= 0) & (tm + ahead < n_tm)

    feat_load = pltpu.make_async_copy(feat_hbm, x_ref, load_sem.at[0])
    feat_load.start()
    w_load = [
        pltpu.make_async_copy(w_hbm, w_raw.at[layer], load_sem.at[1 + layer])
        for layer, w_hbm in enumerate((w1_hbm, w2_hbm))
    ]
    for load in w_load:
        load.start()

    barrier = pltpu.get_barrier_semaphore()
    expected = jnp.int32(n_rc - 1 + n_tm - 1)

    def greet_rc(i):
        other = lax.rem(rc + 1 + i, n_rc)
        pl.semaphore_signal(
            barrier, inc=1, device_id=(tm, other // n_col, lax.rem(other, n_col)), device_id_type=MESH
        )

    def greet_tm(i):
        pl.semaphore_signal(
            barrier, inc=1, device_id=(lax.rem(tm + 1 + i, n_tm), row, col), device_id_type=MESH
        )

    repeat(n_rc - 1, greet_rc)
    repeat(n_tm - 1, greet_tm)
    for ahead in (-1, 1):
        for down in (-1, 0, 1):
            for right in (-1, 0, 1):
                if (down, right) == (0, 0):
                    continue
                here = exists(ahead, down, right)
                expected = expected + here.astype(jnp.int32)

                @pl.when(here)
                def _():
                    pl.semaphore_signal(
                        barrier, inc=1, device_id=(tm + ahead, row + down, col + right), device_id_type=MESH
                    )

    def halo_copy(layer, source, k):
        ahead, down, right = STEPS[k]
        if (down, right) == (0, 0):
            src, dst = source, front.at[layer]
        elif right == 0:
            side = (1 - down) // 2
            src = source.at[:, height - 1 if down == 1 else 0]
            dst = got_rows.at[layer, ahead, side]
        elif down == 0:
            side = (1 - right) // 2
            src = edge_cols.at[layer, side]
            dst = got_cols.at[layer, ahead, side]
        else:
            r_side, c_side = (1 - down) // 2, (1 - right) // 2
            src = corners.at[layer, r_side, c_side]
            dst = got_corners.at[layer, ahead, r_side, c_side]
        return pltpu.make_async_remote_copy(
            src_ref=src,
            dst_ref=dst,
            send_sem=halo_send.at[layer, k],
            recv_sem=halo_recv.at[layer, k],
            device_id=(tm + ahead, row + down, col + right),
            device_id_type=MESH,
        )

    def for_sends(layer, source, act, chosen=lambda step: True):
        for k, step in enumerate(STEPS):
            if chosen(step):

                @pl.when(exists(*step))
                def _():
                    act(halo_copy(layer, source, k))

    def wait_halo(layer, source, ahead):
        for k, step in enumerate(STEPS):
            if step[0] == ahead:

                @pl.when(exists(-step[0], -step[1], -step[2]))
                def _():
                    halo_copy(layer, source, k).wait_recv()

    def pack_edges(layer, source):
        for r_side in range(2):
            for c_side in range(2):
                corners[layer, r_side, c_side] = jnp.zeros((8, channels), F32)
        for frame in range(frames):
            for c_side, w in ((0, width - 1), (1, 0)):
                for h in range(height):
                    line = source[frame, h, w : w + 1, :]
                    edge_cols[layer, c_side, frame, h : h + 1, :] = line
                    if h in (0, height - 1):
                        corners[layer, 0 if h else 1, c_side, frame : frame + 1, :] = line

    def a_copy(layer, i):
        other = lax.rem(rc + 1 + i, n_rc)
        return pltpu.make_async_remote_copy(
            src_ref=stat_a.at[layer, rc],
            dst_ref=stat_a.at[layer, rc],
            send_sem=a_send.at[layer, i],
            recv_sem=a_recv.at[layer, rc],
            device_id=(tm, other // n_col, lax.rem(other, n_col)),
            device_id_type=MESH,
        )

    def a_wait(layer, i):
        other = lax.rem(rc + 1 + i, n_rc)
        pltpu.make_async_remote_copy(
            src_ref=stat_a.at[layer, other],
            dst_ref=stat_a.at[layer, other],
            send_sem=a_send.at[layer, i],
            recv_sem=a_recv.at[layer, other],
            device_id=(tm, other // n_col, lax.rem(other, n_col)),
            device_id_type=MESH,
        ).wait_recv()

    def b_copy(layer, i):
        return pltpu.make_async_remote_copy(
            src_ref=stat_b.at[layer, tm],
            dst_ref=stat_b.at[layer, tm],
            send_sem=b_send.at[layer, i],
            recv_sem=b_recv.at[layer, tm],
            device_id=(lax.rem(tm + 1 + i, n_tm), row, col),
            device_id_type=MESH,
        )

    def b_wait(layer, i):
        other = lax.rem(tm + 1 + i, n_tm)
        pltpu.make_async_remote_copy(
            src_ref=stat_b.at[layer, other],
            dst_ref=stat_b.at[layer, other],
            send_sem=b_send.at[layer, i],
            recv_sem=b_recv.at[layer, other],
            device_id=(other, row, col),
            device_id_type=MESH,
        ).wait_recv()

    tile_row = lax.broadcasted_iota(jnp.int32, (8, channels), 0)

    def tile(mean, spread):
        return jnp.where(tile_row == 0, mean, jnp.where(tile_row == 1, spread, 0.0))

    def local_stats(layer, source):
        values = source[...].reshape(cells, channels)
        mean = jnp.sum(values, axis=0, keepdims=True) * (1.0 / cells)
        centered = values - mean
        stat_a[layer, rc] = tile(mean, jnp.sum(centered * centered, axis=0, keepdims=True))

    def joined(block, entry_count, per_lane):
        shares = block.shape[0]
        total = jnp.sum(block, axis=0)
        center = jnp.broadcast_to(total[0:1], (8, channels))
        center = group_total(center) * (1.0 / (shares * per_group)) if per_lane else center * (1.0 / shares)
        away = block - center[None]
        away = jnp.sum(away * away, axis=0)
        spread = jnp.broadcast_to(total[1:2] + entry_count * away[0:1], (8, channels))
        return center, (group_total(spread) if per_lane else spread)

    def convert(layer):
        w_load[layer].wait()
        piece = channels

        def body(i, _):
            at = pl.ds(pl.multiple_of(i * piece, piece), piece)
            for dt in range(3):
                w_high, w_low = split(w_raw[layer, dt, at, :])
                w_split[layer, dt, at, 0:channels] = w_high
                w_split[layer, dt, at, channels:] = w_low
            return 0

        lax.fori_loop(0, 9, body, 0)

    column = lax.broadcasted_iota(jnp.int32, (height, width, channels), 1)

    def store_taps(frame, first, value, left, right):
        rows = value.shape[0]
        at = column[:rows]
        before = jnp.where(at == 0, left[:, None, :], pltpu.roll(value, 1, 1))
        after = jnp.where(at == width - 1, right[:, None, :], pltpu.roll(value, width - 1, 1))
        for j, shifted in enumerate((before, value, after)):
            v_high, v_low = split(shifted)
            high[frame, first : first + rows, :, j * channels : (j + 1) * channels] = v_high
            low[frame, first : first + rows, :, j * channels : (j + 1) * channels] = v_low

    def spread_frame(layer, source, ahead, frame, activate):
        to = frame + frames * (1 - ahead)

        def valid(down, right, value):
            return jnp.where(exists(-ahead, -down, -right), value, 0.0)

        left = valid(0, 1, activate(got_cols[layer, ahead, 0, frame]))
        right = valid(0, -1, activate(got_cols[layer, ahead, 1, frame]))
        store_taps(to, 1, activate(source[frame]), left, right)
        for side, down in ((0, 1), (1, -1)):
            line = valid(down, 0, activate(got_rows[layer, ahead, side, frame]))
            left = valid(down, 1, activate(got_corners[layer, ahead, side, 0, frame : frame + 1]))
            right = valid(down, -1, activate(got_corners[layer, ahead, side, 1, frame : frame + 1]))
            store_taps(to, 0 if side == 0 else height + 1, line[None], left, right)

    def lines(array, frame):
        return jnp.concatenate(
            [array[frame, dh : dh + height].reshape(height * width, 3 * channels) for dh in range(3)], axis=1
        )

    def dot(a, b):
        return jnp.dot(a, b, preferred_element_type=F32)

    def fold(value):
        return value[:, :channels] + value[:, channels:]

    def conv_half(layer, near, pair, far, dt_near_first):
        w = [w_split.at[layer, dt] for dt in range(3)]
        h_pair, l_pair = lines(high, pair), lines(low, pair)
        h_far, l_far = lines(high, far), lines(low, far)
        first, second = (2, 1) if near else (1, 0)
        only = 2 if near else 0
        both = dot(l_pair, jnp.concatenate([w[first][:, :channels], w[second][:, :channels]], axis=1))
        out_first = fold(dot(h_pair, w[first][...])) + both[:, :channels]
        out_second = fold(dot(h_pair, w[second][...])) + both[:, channels:]
        rest = fold(dot(h_far, w[only][...])) + dot(l_far, w[only][:, :channels])
        if near:
            return out_first, out_second + rest
        return out_first + rest, out_second

    pair_cells = height * width

    def layer_pass(layer, source, gain, shift, before_stats):
        local_stats(layer, source)
        pack_edges(layer, source)
        before_stats()
        repeat(n_rc - 1, lambda i: a_copy(layer, i).start())
        for_sends(layer, source, lambda c: c.start(), lambda s: s[0] == 0)
        for_sends(layer, source, lambda c: c.start(), lambda s: s[0] == 1)
        convert(layer)
        repeat(n_rc - 1, lambda i: a_wait(layer, i))
        center, spread = joined(stat_a[layer], float(cells), True)
        stat_b[layer, tm] = tile(center[0:1], spread[0:1])
        repeat(n_tm - 1, lambda i: b_copy(layer, i).start())
        repeat(n_tm - 1, lambda i: b_wait(layer, i))
        each = float(cells * n_rc * per_group)
        center, spread = joined(stat_b[layer], each, False)
        center = center[0:1]
        scale = lax.rsqrt(spread[0:1] * (1.0 / (each * n_tm)) + epsilon)

        def activate(value):
            lead = (1,) * (value.ndim - 2) + (1, channels)
            u = (value - center.reshape(lead)) * scale.reshape(lead) * gain[...].reshape(lead)
            u = u + shift[...].reshape(lead)
            return u / (1.0 + jnp.exp(-u))

        wait_halo(layer, source, 0)
        for frame in range(frames):
            spread_frame(layer, source, 0, frame, activate)
        first, second = conv_half(layer, True, 2, 3, None)
        part[0], part[1] = first, second

        wait_halo(layer, source, 1)

        @pl.when(tm == 0)
        def _():
            for to in range(2):
                high[to] = high[2]
                low[to] = low[2]

        @pl.when(tm != 0)
        def _():
            for frame in range(frames):
                spread_frame(layer, front.at[layer], 1, frame, activate)

        first, second = conv_half(layer, False, 1, 0, None)
        return part[0] + first, part[1] + second

    feat_load.wait()
    pair = layer_pass(0, x_ref, gain1, shift1, lambda: pl.semaphore_wait(barrier, expected))
    for frame in range(frames):
        hid_ref[frame] = pair[frame].reshape(height, width, channels)
    pair = layer_pass(1, hid_ref, gain2, shift2, lambda: None)
    for frame in range(frames):
        moved = pair[frame].reshape(height, width, channels)
        out_ref[frame] = x_ref[frame] + moved + bias[...].reshape(1, 1, channels)

    for layer, source in enumerate((x_ref, hid_ref)):
        repeat(n_rc - 1, lambda i: a_copy(layer, i).wait_send())
        repeat(n_tm - 1, lambda i: b_copy(layer, i).wait_send())
        for_sends(layer, source, lambda c: c.wait_send())


def local(counts, features, gain1, shift1, weight1, gain2, shift2, weight2, bias):
    n_tm, n_row, n_col = counts
    frames, height, width, channels = features.shape
    taps = 9 * channels
    n_rc = n_row * n_col
    lane = lambda v: v.reshape(1, channels)
    weights = lambda w: w.reshape(3, taps, channels)
    vmem = pl.BlockSpec(memory_space=pltpu.VMEM)
    hbm = pl.BlockSpec(memory_space=pl.ANY)
    padded = (2 * frames, height + 2, width, 3 * channels)
    dma = pltpu.SemaphoreType.DMA
    return pl.pallas_call(
        functools.partial(kernel, counts),
        out_shape=jax.ShapeDtypeStruct(features.shape, F32),
        in_specs=[hbm, vmem, vmem, hbm, vmem, vmem, hbm, vmem],
        out_specs=vmem,
        scratch_shapes=[
            pltpu.VMEM(features.shape, F32),
            pltpu.VMEM(features.shape, F32),
            pltpu.VMEM((2, 3, taps, channels), F32),
            pltpu.VMEM((2, 3, taps, 2 * channels), BF16),
            pltpu.VMEM(padded, BF16),
            pltpu.VMEM(padded, BF16),
            pltpu.VMEM((2, height * width, channels), F32),
            pltpu.VMEM((2, 2, frames, height, channels), F32),
            pltpu.VMEM((2, 2, 2, 8, channels), F32),
            pltpu.VMEM((2, *features.shape), F32),
            pltpu.VMEM((2, 2, 2, frames, width, channels), F32),
            pltpu.VMEM((2, 2, 2, frames, height, channels), F32),
            pltpu.VMEM((2, 2, 2, 2, 8, channels), F32),
            pltpu.VMEM((2, n_rc, 8, channels), F32),
            pltpu.VMEM((2, n_tm, 8, channels), F32),
            dma((3,)),
            dma((2, len(STEPS))),
            dma((2, len(STEPS))),
            dma((2, max(1, n_rc - 1))),
            dma((2, n_rc)),
            dma((2, max(1, n_tm - 1))),
            dma((2, n_tm)),
        ],
        compiler_params=pltpu.CompilerParams(
            collective_id=0, has_side_effects=True, vmem_limit_bytes=40 * 1024 * 1024
        ),
    )(features, lane(gain1), lane(shift1), weights(weight1), lane(gain2), lane(shift2), weights(weight2), lane(bias))


def solution(mesh):
    counts = tuple(mesh.shape[axis] for axis in ("tm", "row", "col"))
    in_specs = (P("tm", "row", "col", None), P(), P(), P(), P(), P(), P(), P())
    out_specs = P("tm", "row", "col", None)
    return jax.shard_map(
        functools.partial(local, counts), mesh=mesh, in_specs=in_specs, out_specs=out_specs, check_vma=False
    )
```

```python
import functools
import jax
import jax.numpy as jnp
from jax import lax
from jax.experimental import pallas as pl
from jax.experimental.pallas import tpu as pltpu
from jax.sharding import PartitionSpec as P

GROUPS = 32
MESH = pl.DeviceIdType.MESH
epsilon = 1e-06
F32 = jnp.float32
BF16 = jnp.bfloat16
STEPS = [
    (ahead, down, right)
    for ahead in (0, 1)
    for down in (-1, 0, 1)
    for right in (-1, 0, 1)
    if (down, right) != (0, 0)
]


def repeat(count, body):
    if count <= 4:
        for i in range(count):
            body(i)
    else:
        lax.fori_loop(0, count, lambda i, _: (body(i), 0)[1], 0)


def group_total(value):
    channels = value.shape[-1]
    lane = lax.broadcasted_iota(jnp.int32, value.shape, 1)
    step = 1
    while step < channels // GROUPS:
        upper = pltpu.roll(value, channels - step, 1)
        lower = pltpu.roll(value, step, 1)
        value = value + jnp.where((lane & step) == 0, upper, lower)
        step *= 2
    return value


def split(value):
    high = value.astype(BF16)
    return high, (value - high.astype(F32)).astype(BF16)


def kernel(
    counts,
    feat_hbm, gain1_hbm, shift1_hbm, w1_hbm, gain2_hbm, shift2_hbm, w2_hbm, bias_hbm,
    out_ref,
    lanes,
    x_ref, hid_ref, w_raw, w_split, high, low, part,
    edge_cols, corners, front, got_rows, got_cols, got_corners, stats,
    load_sem, halo_send, halo_recv, front_send, front_recv, stat_send, stat_recv,
):
    n_tm, n_row, n_col = counts
    n_all = n_tm * n_row * n_col
    tm, row, col = lax.axis_index("tm"), lax.axis_index("row"), lax.axis_index("col")
    rank = (tm * n_row + row) * n_col + col
    frames, height, width, channels = x_ref.shape
    cells = frames * height * width
    per_group = channels // GROUPS

    def place(index):
        return index // (n_row * n_col), lax.rem(index // n_col, n_row), lax.rem(index, n_col)

    def exists(ahead, down, right):
        ok = (row + down >= 0) & (row + down < n_row)
        ok = ok & (col + right >= 0) & (col + right < n_col)
        return ok & (tm + ahead >= 0) & (tm + ahead < n_tm)

    feat_load = pltpu.make_async_copy(feat_hbm, x_ref, load_sem.at[0])
    feat_load.start()
    w_load = [
        pltpu.make_async_copy(w_hbm, w_raw.at[layer], load_sem.at[1 + layer])
        for layer, w_hbm in enumerate((w1_hbm, w2_hbm))
    ]
    lane_hbm = (gain1_hbm, shift1_hbm, gain2_hbm, shift2_hbm, bias_hbm)
    lane_load = [pltpu.make_async_copy(v, lanes.at[i], load_sem.at[3 + i]) for i, v in enumerate(lane_hbm)]
    gain1, shift1, gain2, shift2, bias = [lanes.at[i] for i in range(5)]
    for load in (*w_load, *lane_load):
        load.start()

    barrier = pltpu.get_barrier_semaphore()

    def greet(i):
        pl.semaphore_signal(
            barrier, inc=1, device_id=place(lax.rem(rank + 1 + i, n_all)), device_id_type=MESH
        )

    repeat(n_all - 1, greet)

    def halo_copy(layer, source, k):
        ahead, down, right = STEPS[k]
        if right == 0:
            side = (1 - down) // 2
            src = source.at[:, height - 1 if down == 1 else 0]
            dst = got_rows.at[layer, ahead, side]
        elif down == 0:
            side = (1 - right) // 2
            src = edge_cols.at[layer, side]
            dst = got_cols.at[layer, ahead, side]
        else:
            r_side, c_side = (1 - down) // 2, (1 - right) // 2
            src = corners.at[layer, r_side, c_side]
            dst = got_corners.at[layer, ahead, r_side, c_side]
        return pltpu.make_async_remote_copy(
            src_ref=src,
            dst_ref=dst,
            send_sem=halo_send.at[layer, k],
            recv_sem=halo_recv.at[layer, k],
            device_id=(tm + ahead, row + down, col + right),
            device_id_type=MESH,
        )

    def front_copy(layer, source, frame):
        return pltpu.make_async_remote_copy(
            src_ref=source.at[frame],
            dst_ref=front.at[layer, frame],
            send_sem=front_send.at[layer, frame],
            recv_sem=front_recv.at[layer, frame],
            device_id=(tm + 1, row, col),
            device_id_type=MESH,
        )

    def send_front(layer, source, frame):
        @pl.when(tm + 1 < n_tm)
        def _():
            front_copy(layer, source, frame).start()

    def for_sends(layer, source, act):
        for k, step in enumerate(STEPS):


            @pl.when(exists(*step))
            def _():
                act(halo_copy(layer, source, k))

    def wait_halo(layer, source, ahead):
        for k, step in enumerate(STEPS):
            if step[0] == ahead:

                @pl.when(exists(-step[0], -step[1], -step[2]))
                def _():
                    halo_copy(layer, source, k).wait_recv()

    def pack_edges(layer, source):
        for r_side in range(2):
            for c_side in range(2):
                corners[layer, r_side, c_side] = jnp.zeros((8, channels), F32)
        for frame in range(frames):
            for c_side, w in ((0, width - 1), (1, 0)):
                for h in range(height):
                    line = source[frame, h, w : w + 1, :]
                    edge_cols[layer, c_side, frame, h : h + 1, :] = line
                    if h in (0, height - 1):
                        corners[layer, 0 if h else 1, c_side, frame : frame + 1, :] = line

    def stat_copy(layer, i):
        to = lax.rem(rank + 1 + i, n_all)
        return pltpu.make_async_remote_copy(
            src_ref=stats.at[layer, rank],
            dst_ref=stats.at[layer, rank],
            send_sem=stat_send.at[layer],
            recv_sem=stat_recv.at[layer],
            device_id=place(to),
            device_id_type=MESH,
        )

    def stat_wait(layer):
        others = stats.at[layer, pl.ds(0, n_all - 1)]
        return pltpu.make_async_remote_copy(
            src_ref=others,
            dst_ref=others,
            send_sem=stat_send.at[layer],
            recv_sem=stat_recv.at[layer],
            device_id=place(lax.rem(rank + 1, n_all)),
            device_id_type=MESH,
        )

    def local_stats(layer, source):
        values = source[...].reshape(cells, channels)
        mean = jnp.sum(values, axis=0, keepdims=True) * (1.0 / cells)
        centered = values - mean
        stats[layer, rank, 0:1] = mean
        stats[layer, rank, 1:2] = jnp.sum(centered * centered, axis=0, keepdims=True)

    def joined(layer):
        block = stats[layer]
        total = jnp.sum(block, axis=0)
        center = jnp.broadcast_to(total[0:1], (8, channels))
        center = group_total(center)[0:1] * (1.0 / (n_all * per_group))
        away = block[:, 0:1, :] - center[None]
        spread = total[1:2] + float(cells) * jnp.sum(away * away, axis=0)
        spread = group_total(jnp.broadcast_to(spread, (8, channels)))[0:1]
        return center, spread * (1.0 / (float(cells) * n_all * per_group))

    def convert(layer):
        w_load[layer].wait()
        piece = channels

        def body(i, _):
            at = pl.ds(pl.multiple_of(i * piece, piece), piece)
            for dt in range(3):
                w_high, w_low = split(w_raw[layer, dt, at, :])
                w_split[layer, dt, at, 0:channels] = w_high
                w_split[layer, dt, at, channels:] = w_low
            return 0

        lax.fori_loop(0, 9, body, 0)

    column = lax.broadcasted_iota(jnp.int32, (height, width, channels), 1)

    def store_taps(frame, first, value, left, right):
        rows = value.shape[0]
        at = column[:rows]
        before = jnp.where(at == 0, left[:, None, :], pltpu.roll(value, 1, 1))
        after = jnp.where(at == width - 1, right[:, None, :], pltpu.roll(value, width - 1, 1))
        for j, shifted in enumerate((before, value, after)):
            v_high, v_low = split(shifted)
            high[frame, first : first + rows, :, j * channels : (j + 1) * channels] = v_high
            low[frame, first : first + rows, :, j * channels : (j + 1) * channels] = v_low

    def spread_frame(layer, source, ahead, frame, activate):
        to = frame + frames * (1 - ahead)

        def valid(down, right, value):
            return jnp.where(exists(-ahead, -down, -right), value, 0.0)

        left = valid(0, 1, activate(got_cols[layer, ahead, 0, frame]))
        right = valid(0, -1, activate(got_cols[layer, ahead, 1, frame]))
        store_taps(to, 1, activate(source[frame]), left, right)
        for side, down in ((0, 1), (1, -1)):
            line = valid(down, 0, activate(got_rows[layer, ahead, side, frame]))
            left = valid(down, 1, activate(got_corners[layer, ahead, side, 0, frame : frame + 1]))
            right = valid(down, -1, activate(got_corners[layer, ahead, side, 1, frame : frame + 1]))
            store_taps(to, 0 if side == 0 else height + 1, line[None], left, right)

    def lines(array, frame):
        return jnp.concatenate(
            [array[frame, dh : dh + height].reshape(height * width, 3 * channels) for dh in range(3)], axis=1
        )

    def dot(a, b):
        return jnp.dot(a, b, preferred_element_type=F32)

    def fold(value):
        return value[:, :channels] + value[:, channels:]

    def conv_pair(layer, frame, near):
        w = [w_split.at[layer, dt] for dt in range(3)]
        first, second = (2, 1) if near else (1, 0)
        h, l = lines(high, frame), lines(low, frame)
        both = dot(l, jnp.concatenate([w[first][:, :channels], w[second][:, :channels]], axis=1))
        out_second = fold(dot(h, w[second][...])) + both[:, channels:]
        return fold(dot(h, w[first][...])) + both[:, :channels], out_second

    def conv_one(layer, frame, dt):
        w = w_split.at[layer, dt]
        return fold(dot(lines(high, frame), w[...])) + dot(lines(low, frame), w[:, :channels])

    def start_stats(layer):
        repeat(n_all - 1, lambda i: stat_copy(layer, i).start())

    def layer_pass(layer, source, gain, shift, beside, emit):
        if layer == 0:
            convert(0)
        stat_wait(layer).wait_recv()
        center, spread = joined(layer)
        scale = lax.rsqrt(spread + epsilon)

        def activate(value):
            lead = (1,) * (value.ndim - 2) + (1, channels)
            u = (value - center.reshape(lead)) * scale.reshape(lead) * gain[...].reshape(lead)
            u = u + shift[...].reshape(lead)
            return u / (1.0 + jnp.exp(-u))

        wait_halo(layer, source, 0)
        for frame in range(frames):
            spread_frame(layer, source, 0, frame, activate)
        part[0], part[1] = conv_pair(layer, 2, True)
        part[1] += conv_one(layer, 3, 2)
        beside()
        wait_halo(layer, source, 1)

        def arrived(frame):
            @pl.when(tm == 0)
            def _():
                high[frame] = high[2]
                low[frame] = low[2]

            @pl.when(tm != 0)
            def _():
                front_copy(layer, source, frame).wait_recv()
                spread_frame(layer, front.at[layer], 1, frame, activate)

        arrived(1)
        first, second = conv_pair(layer, 1, False)
        part[0] += first
        emit(1, part[1] + second)
        arrived(0)
        emit(0, part[0] + conv_one(layer, 0, 0))

    def keep_hidden(frame, value):
        hid_ref[frame] = value.reshape(height, width, channels)
        send_front(1, hid_ref, frame)

    def keep_output(frame, value):
        moved = value.reshape(height, width, channels)
        out_ref[frame] = x_ref[frame] + moved + bias[...].reshape(1, 1, channels)

    feat_load.wait()
    for load in lane_load:
        load.wait()
    local_stats(0, x_ref)
    pack_edges(0, x_ref)
    pl.semaphore_wait(barrier, n_all - 1)
    for_sends(0, x_ref, lambda c: c.start())
    start_stats(0)
    send_front(0, x_ref, 1)
    send_front(0, x_ref, 0)
    layer_pass(0, x_ref, gain1, shift1, lambda: convert(1), keep_hidden)
    local_stats(1, hid_ref)
    start_stats(1)
    pack_edges(1, hid_ref)
    for_sends(1, hid_ref, lambda c: c.start())
    layer_pass(1, hid_ref, gain2, shift2, lambda: None, keep_output)

    for layer, source in enumerate((x_ref, hid_ref)):
        stat_wait(layer).wait_send()
        for_sends(layer, source, lambda c: c.wait_send())

        @pl.when(tm + 1 < n_tm)
        def _():
            for frame in range(frames):
                front_copy(layer, source, frame).wait_send()


def local(counts, features, gain1, shift1, weight1, gain2, shift2, weight2, bias):
    n_tm, n_row, n_col = counts
    frames, height, width, channels = features.shape
    taps = 9 * channels
    lane = lambda v: v.reshape(1, channels)
    weights = lambda w: w.reshape(3, taps, channels)
    vmem = pl.BlockSpec(memory_space=pltpu.VMEM)
    hbm = pl.BlockSpec(memory_space=pltpu.HBM)
    padded = (2 * frames, height + 2, width, 3 * channels)
    dma = pltpu.SemaphoreType.DMA
    return pl.pallas_call(
        functools.partial(kernel, counts),
        out_shape=jax.ShapeDtypeStruct(features.shape, F32),
        in_specs=[hbm] * 8,
        out_specs=vmem,
        scratch_shapes=[
            pltpu.VMEM((5, 1, channels), F32),
            pltpu.VMEM(features.shape, F32),
            pltpu.VMEM(features.shape, F32),
            pltpu.VMEM((2, 3, taps, channels), F32),
            pltpu.VMEM((2, 3, taps, 2 * channels), BF16),
            pltpu.VMEM(padded, BF16),
            pltpu.VMEM(padded, BF16),
            pltpu.VMEM((2, height * width, channels), F32),
            pltpu.VMEM((2, 2, frames, height, channels), F32),
            pltpu.VMEM((2, 2, 2, 8, channels), F32),
            pltpu.VMEM((2, *features.shape), F32),
            pltpu.VMEM((2, 2, 2, frames, width, channels), F32),
            pltpu.VMEM((2, 2, 2, frames, height, channels), F32),
            pltpu.VMEM((2, 2, 2, 2, 8, channels), F32),
            pltpu.VMEM((2, n_tm * n_row * n_col, 2, channels), F32),
            dma((8,)),
            dma((2, len(STEPS))),
            dma((2, len(STEPS))),
            dma((2, frames)),
            dma((2, frames)),
            dma((2,)),
            dma((2,)),
        ],
        compiler_params=pltpu.CompilerParams(
            collective_id=0, has_side_effects=True, vmem_limit_bytes=60 * 1024 * 1024
        ),
    )(features, lane(gain1), lane(shift1), weights(weight1), lane(gain2), lane(shift2), weights(weight2), lane(bias))


def solution(mesh):
    counts = tuple(mesh.shape[axis] for axis in ("tm", "row", "col"))
    in_specs = (P("tm", "row", "col", None), P(), P(), P(), P(), P(), P(), P())
    out_specs = P("tm", "row", "col", None)
    return jax.shard_map(
        functools.partial(local, counts), mesh=mesh, in_specs=in_specs, out_specs=out_specs, check_vma=False
    )
```

```python
import functools
import jax
import jax.numpy as jnp
from jax import lax
from jax.experimental import pallas as pl
from jax.experimental.pallas import tpu as pltpu
from jax.sharding import PartitionSpec as P

GROUPS = 32
MESH = pl.DeviceIdType.MESH
epsilon = 1e-06
F32 = jnp.float32
BF16 = jnp.bfloat16
STEPS = [
    (ahead, down, right)
    for ahead in (0, 1)
    for down in (-1, 0, 1)
    for right in (-1, 0, 1)
    if (down, right) != (0, 0)
]


def repeat(count, body):
    if count <= 4:
        for i in range(count):
            body(i)
    else:
        lax.fori_loop(0, count, lambda i, _: (body(i), 0)[1], 0)


def group_total(value):
    channels = value.shape[-1]
    lane = lax.broadcasted_iota(jnp.int32, value.shape, 1)
    step = 1
    while step < channels // GROUPS:
        upper = pltpu.roll(value, channels - step, 1)
        lower = pltpu.roll(value, step, 1)
        value = value + jnp.where((lane & step) == 0, upper, lower)
        step *= 2
    return value


def split(value):
    high = value.astype(BF16)
    return high, (value - high.astype(F32)).astype(BF16)


def kernel(
    counts,
    feat_hbm, gain1_hbm, shift1_hbm, w1_hbm, gain2_hbm, shift2_hbm, w2_hbm, bias_hbm,
    out_ref,
    lanes,
    x_ref, hid_ref, w_raw, w_split, high, low, part,
    edge_cols, corners, front, got_rows, got_cols, got_corners, stats,
    load_sem, halo_send, halo_recv, front_send, front_recv, stat_send, stat_recv,
):
    n_tm, n_row, n_col = counts
    n_all = n_tm * n_row * n_col
    tm, row, col = lax.axis_index("tm"), lax.axis_index("row"), lax.axis_index("col")
    rank = (tm * n_row + row) * n_col + col
    frames, height, width, channels = x_ref.shape
    cells = frames * height * width
    per_group = channels // GROUPS

    def place(index):
        return index // (n_row * n_col), lax.rem(index // n_col, n_row), lax.rem(index, n_col)

    def exists(ahead, down, right):
        ok = (row + down >= 0) & (row + down < n_row)
        ok = ok & (col + right >= 0) & (col + right < n_col)
        return ok & (tm + ahead >= 0) & (tm + ahead < n_tm)

    feat_load = pltpu.make_async_copy(feat_hbm, x_ref, load_sem.at[0])
    feat_load.start()
    w_load = [
        pltpu.make_async_copy(w_hbm, w_raw.at[layer], load_sem.at[1 + layer])
        for layer, w_hbm in enumerate((w1_hbm, w2_hbm))
    ]
    lane_hbm = (gain1_hbm, shift1_hbm, gain2_hbm, shift2_hbm, bias_hbm)
    lane_load = [pltpu.make_async_copy(v, lanes.at[i], load_sem.at[3 + i]) for i, v in enumerate(lane_hbm)]
    gain1, shift1, gain2, shift2, bias = [lanes.at[i] for i in range(5)]
    for load in (*w_load, *lane_load):
        load.start()

    barrier = pltpu.get_barrier_semaphore()

    def greet(i):
        pl.semaphore_signal(
            barrier, inc=1, device_id=place(lax.rem(rank + 1 + i, n_all)), device_id_type=MESH
        )

    repeat(n_all - 1, greet)

    def halo_copy(layer, source, k):
        ahead, down, right = STEPS[k]
        if right == 0:
            side = (1 - down) // 2
            src = source.at[:, height - 1 if down == 1 else 0]
            dst = got_rows.at[layer, ahead, side]
        elif down == 0:
            side = (1 - right) // 2
            src = edge_cols.at[layer, side]
            dst = got_cols.at[layer, ahead, side]
        else:
            r_side, c_side = (1 - down) // 2, (1 - right) // 2
            src = corners.at[layer, r_side, c_side]
            dst = got_corners.at[layer, ahead, r_side, c_side]
        return pltpu.make_async_remote_copy(
            src_ref=src,
            dst_ref=dst,
            send_sem=halo_send.at[layer, k],
            recv_sem=halo_recv.at[layer, k],
            device_id=(tm + ahead, row + down, col + right),
            device_id_type=MESH,
        )

    def front_copy(layer, source, frame):
        return pltpu.make_async_remote_copy(
            src_ref=source.at[frame],
            dst_ref=front.at[layer, frame],
            send_sem=front_send.at[layer, frame],
            recv_sem=front_recv.at[layer, frame],
            device_id=(tm + 1, row, col),
            device_id_type=MESH,
        )

    def send_front(layer, source, frame):
        @pl.when(tm + 1 < n_tm)
        def _():
            front_copy(layer, source, frame).start()

    def for_sends(layer, source, act):
        for k, step in enumerate(STEPS):

            @pl.when(exists(*step))
            def _():
                act(halo_copy(layer, source, k))

    def wait_halo(layer, source, ahead):
        for k, step in enumerate(STEPS):
            if step[0] == ahead:

                @pl.when(exists(-step[0], -step[1], -step[2]))
                def _():
                    halo_copy(layer, source, k).wait_recv()

    def pack_edges(layer, source):
        for r_side in range(2):
            for c_side in range(2):
                corners[layer, r_side, c_side] = jnp.zeros((8, channels), F32)
        for frame in range(frames):
            for c_side, w in ((0, width - 1), (1, 0)):
                for h in range(height):
                    line = source[frame, h, w : w + 1, :]
                    edge_cols[layer, c_side, frame, h : h + 1, :] = line
                    if h in (0, height - 1):
                        corners[layer, 0 if h else 1, c_side, frame : frame + 1, :] = line

    def stat_copy(layer, i):
        to = lax.rem(rank + 1 + i, n_all)
        return pltpu.make_async_remote_copy(
            src_ref=stats.at[layer, rank],
            dst_ref=stats.at[layer, rank],
            send_sem=stat_send.at[layer],
            recv_sem=stat_recv.at[layer],
            device_id=place(to),
            device_id_type=MESH,
        )

    def stat_wait(layer):
        others = stats.at[layer, pl.ds(0, n_all - 1)]
        return pltpu.make_async_remote_copy(
            src_ref=others,
            dst_ref=others,
            send_sem=stat_send.at[layer],
            recv_sem=stat_recv.at[layer],
            device_id=place(lax.rem(rank + 1, n_all)),
            device_id_type=MESH,
        )

    def local_stats(layer, source):
        values = source[...].reshape(cells, channels)
        mean = jnp.sum(values, axis=0, keepdims=True) * (1.0 / cells)
        centered = values - mean
        stats[layer, rank, 0:1] = mean
        stats[layer, rank, 1:2] = jnp.sum(centered * centered, axis=0, keepdims=True)

    def joined(layer):
        block = stats[layer]
        total = jnp.sum(block, axis=0)
        center = jnp.broadcast_to(total[0:1], (8, channels))
        center = group_total(center)[0:1] * (1.0 / (n_all * per_group))
        away = block[:, 0:1, :] - center[None]
        spread = total[1:2] + float(cells) * jnp.sum(away * away, axis=0)
        spread = group_total(jnp.broadcast_to(spread, (8, channels)))[0:1]
        return center, spread * (1.0 / (float(cells) * n_all * per_group))

    def convert(layer):
        w_load[layer].wait()
        piece = channels

        def body(i, _):
            at = pl.ds(pl.multiple_of(i * piece, piece), piece)
            for dt in range(3):
                w_high, w_low = split(w_raw[layer, dt, at, :])
                w_split[layer, dt, at, 0:channels] = w_high
                w_split[layer, dt, at, channels:] = w_low
            return 0

        lax.fori_loop(0, 9, body, 0)

    column = lax.broadcasted_iota(jnp.int32, (height, width, channels), 1)

    def store_taps(frame, first, value, left, right):
        rows = value.shape[0]
        at = column[:rows]
        before = jnp.where(at == 0, left[:, None, :], pltpu.roll(value, 1, 1))
        after = jnp.where(at == width - 1, right[:, None, :], pltpu.roll(value, width - 1, 1))
        for j, shifted in enumerate((before, value, after)):
            v_high, v_low = split(shifted)
            high[frame, first : first + rows, :, j * channels : (j + 1) * channels] = v_high
            low[frame, first : first + rows, :, j * channels : (j + 1) * channels] = v_low

    def spread_frame(layer, source, ahead, frame, activate):
        to = frame + frames * (1 - ahead)

        def valid(down, right, value):
            return jnp.where(exists(-ahead, -down, -right), value, 0.0)

        left = valid(0, 1, activate(got_cols[layer, ahead, 0, frame]))
        right = valid(0, -1, activate(got_cols[layer, ahead, 1, frame]))
        store_taps(to, 1, activate(source[frame]), left, right)
        for side, down in ((0, 1), (1, -1)):
            line = valid(down, 0, activate(got_rows[layer, ahead, side, frame]))
            left = valid(down, 1, activate(got_corners[layer, ahead, side, 0, frame : frame + 1]))
            right = valid(down, -1, activate(got_corners[layer, ahead, side, 1, frame : frame + 1]))
            store_taps(to, 0 if side == 0 else height + 1, line[None], left, right)

    def lines(array, frame):
        return jnp.concatenate(
            [array[frame, dh : dh + height].reshape(height * width, 3 * channels) for dh in range(3)], axis=1
        )

    def dot(a, b):
        return jnp.dot(a, b, preferred_element_type=F32)

    def fold(value):
        return value[:, :channels] + value[:, channels:]

    def conv_pair(layer, frame, near):
        w = [w_split.at[layer, dt] for dt in range(3)]
        first, second = (2, 1) if near else (1, 0)
        h, l = lines(high, frame), lines(low, frame)
        both = dot(l, jnp.concatenate([w[first][:, :channels], w[second][:, :channels]], axis=1))
        out_second = fold(dot(h, w[second][...])) + both[:, channels:]
        return fold(dot(h, w[first][...])) + both[:, :channels], out_second

    def conv_own(layer):
        w = [w_split.at[layer, dt] for dt in range(3)]
        size = height * width
        first = lines(high, 2)
        shared = fold(dot(jnp.concatenate([first, lines(high, 3)], axis=0), w[2][...]))
        lows = jnp.concatenate([lines(low, 2), lines(low, 3)], axis=0)
        both = dot(lows, jnp.concatenate([w[2][:, :channels], w[1][:, :channels]], axis=1))
        out_second = shared[size:] + fold(dot(first, w[1][...])) + both[:size, channels:] + both[size:, :channels]
        return shared[:size] + both[:size, :channels], out_second

    def conv_one(layer, frame, dt):
        w = w_split.at[layer, dt]
        return fold(dot(lines(high, frame), w[...])) + dot(lines(low, frame), w[:, :channels])

    def start_stats(layer):
        repeat(n_all - 1, lambda i: stat_copy(layer, i).start())

    def layer_pass(layer, source, gain, shift, beside, emit):
        if layer == 0:
            convert(0)
        stat_wait(layer).wait_recv()
        center, spread = joined(layer)
        scale = lax.rsqrt(spread + epsilon)

        def activate(value):
            lead = (1,) * (value.ndim - 2) + (1, channels)
            u = (value - center.reshape(lead)) * scale.reshape(lead) * gain[...].reshape(lead)
            u = u + shift[...].reshape(lead)
            return u / (1.0 + jnp.exp(-u))

        wait_halo(layer, source, 0)
        for frame in range(frames):
            spread_frame(layer, source, 0, frame, activate)
        part[0], part[1] = conv_own(layer)
        beside()
        wait_halo(layer, source, 1)

        def arrived(frame):
            @pl.when(tm == 0)
            def _():
                high[frame] = high[2]
                low[frame] = low[2]

            @pl.when(tm != 0)
            def _():
                front_copy(layer, source, frame).wait_recv()
                spread_frame(layer, front.at[layer], 1, frame, activate)

        arrived(1)
        first, second = conv_pair(layer, 1, False)
        part[0] += first
        emit(1, part[1] + second)
        arrived(0)
        emit(0, part[0] + conv_one(layer, 0, 0))

    def keep_hidden(frame, value):
        hid_ref[frame] = value.reshape(height, width, channels)
        if frame == 1:
            send_front(1, hid_ref, 1)

    def keep_output(frame, value):
        moved = value.reshape(height, width, channels)
        out_ref[frame] = x_ref[frame] + moved + bias[...].reshape(1, 1, channels)

    feat_load.wait()
    for load in lane_load:
        load.wait()
    local_stats(0, x_ref)
    pack_edges(0, x_ref)
    pl.semaphore_wait(barrier, n_all - 1)
    start_stats(0)
    send_front(0, x_ref, 1)
    for_sends(0, x_ref, lambda c: c.start())
    send_front(0, x_ref, 0)
    layer_pass(0, x_ref, gain1, shift1, lambda: convert(1), keep_hidden)
    local_stats(1, hid_ref)
    start_stats(1)
    pack_edges(1, hid_ref)
    for_sends(1, hid_ref, lambda c: c.start())
    send_front(1, hid_ref, 0)
    layer_pass(1, hid_ref, gain2, shift2, lambda: None, keep_output)

    for layer, source in enumerate((x_ref, hid_ref)):
        stat_wait(layer).wait_send()
        for_sends(layer, source, lambda c: c.wait_send())

        @pl.when(tm + 1 < n_tm)
        def _():
            for frame in range(frames):
                front_copy(layer, source, frame).wait_send()


def local(counts, features, gain1, shift1, weight1, gain2, shift2, weight2, bias):
    n_tm, n_row, n_col = counts
    frames, height, width, channels = features.shape
    taps = 9 * channels
    lane = lambda v: v.reshape(1, channels)
    weights = lambda w: w.reshape(3, taps, channels)
    vmem = pl.BlockSpec(memory_space=pltpu.VMEM)
    hbm = pl.BlockSpec(memory_space=pltpu.HBM)
    padded = (2 * frames, height + 2, width, 3 * channels)
    dma = pltpu.SemaphoreType.DMA
    return pl.pallas_call(
        functools.partial(kernel, counts),
        out_shape=jax.ShapeDtypeStruct(features.shape, F32),
        in_specs=[hbm] * 8,
        out_specs=vmem,
        scratch_shapes=[
            pltpu.VMEM((5, 1, channels), F32),
            pltpu.VMEM(features.shape, F32),
            pltpu.VMEM(features.shape, F32),
            pltpu.VMEM((2, 3, taps, channels), F32),
            pltpu.VMEM((2, 3, taps, 2 * channels), BF16),
            pltpu.VMEM(padded, BF16),
            pltpu.VMEM(padded, BF16),
            pltpu.VMEM((2, height * width, channels), F32),
            pltpu.VMEM((2, 2, frames, height, channels), F32),
            pltpu.VMEM((2, 2, 2, 8, channels), F32),
            pltpu.VMEM((2, *features.shape), F32),
            pltpu.VMEM((2, 2, 2, frames, width, channels), F32),
            pltpu.VMEM((2, 2, 2, frames, height, channels), F32),
            pltpu.VMEM((2, 2, 2, 2, 8, channels), F32),
            pltpu.VMEM((2, n_tm * n_row * n_col, 2, channels), F32),
            dma((8,)),
            dma((2, len(STEPS))),
            dma((2, len(STEPS))),
            dma((2, frames)),
            dma((2, frames)),
            dma((2,)),
            dma((2,)),
        ],
        compiler_params=pltpu.CompilerParams(
            collective_id=0, has_side_effects=True, vmem_limit_bytes=60 * 1024 * 1024
        ),
    )(features, lane(gain1), lane(shift1), weights(weight1), lane(gain2), lane(shift2), weights(weight2), lane(bias))


def solution(mesh):
    counts = tuple(mesh.shape[axis] for axis in ("tm", "row", "col"))
    in_specs = (P("tm", "row", "col", None), P(), P(), P(), P(), P(), P(), P())
    out_specs = P("tm", "row", "col", None)
    return jax.shard_map(
        functools.partial(local, counts), mesh=mesh, in_specs=in_specs, out_specs=out_specs, check_vma=False
    )
```

```python
import functools
import itertools
import jax
import jax.numpy as jnp
from jax import lax
from jax.experimental import pallas as pl
from jax.experimental.pallas import tpu as pltpu
from jax.sharding import PartitionSpec as P

GROUPS = 32
MESH = pl.DeviceIdType.MESH
epsilon = 1e-06
F32 = jnp.float32
BF16 = jnp.bfloat16
STEPS = [
    (ahead, down, right)
    for ahead in (0, 1)
    for down in (-1, 0, 1)
    for right in (-1, 0, 1)
    if (down, right) != (0, 0)
]


def group_total(value):
    channels = value.shape[-1]
    lane = lax.broadcasted_iota(jnp.int32, value.shape, 1)
    step = 1
    while step < channels // GROUPS:
        upper = pltpu.roll(value, channels - step, 1)
        lower = pltpu.roll(value, step, 1)
        value = value + jnp.where((lane & step) == 0, upper, lower)
        step *= 2
    return value


def split(value):
    high = value.astype(BF16)
    return high, (value - high.astype(F32)).astype(BF16)


def kernel(
    counts,
    feat_hbm, gain1_hbm, shift1_hbm, w1_hbm, gain2_hbm, shift2_hbm, w2_hbm, bias_hbm,
    out_ref,
    lanes,
    x_ref, hid_ref, w_raw, w_split, high, low, part,
    edge_cols, corners, front, got_rows, got_cols, got_corners, stats,
    load_sem, halo_send, halo_recv, front_send, front_recv, stat_send, stat_recv,
):
    n_tm, n_row, n_col = counts
    n_all = n_tm * n_row * n_col
    tm, row, col = lax.axis_index("tm"), lax.axis_index("row"), lax.axis_index("col")
    rank = (tm * n_row + row) * n_col + col
    frames, height, width, channels = x_ref.shape
    cells = frames * height * width
    per_group = channels // GROUPS

    def place(index):
        return index // (n_row * n_col), lax.rem(index // n_col, n_row), lax.rem(index, n_col)

    def exists(ahead, down, right):
        ok = (row + down >= 0) & (row + down < n_row)
        ok = ok & (col + right >= 0) & (col + right < n_col)
        return ok & (tm + ahead >= 0) & (tm + ahead < n_tm)

    feat_load = pltpu.make_async_copy(feat_hbm, x_ref, load_sem.at[0])
    feat_load.start()
    w_load = [
        pltpu.make_async_copy(w_hbm, w_raw.at[layer], load_sem.at[1 + layer])
        for layer, w_hbm in enumerate((w1_hbm, w2_hbm))
    ]
    lane_hbm = (gain1_hbm, shift1_hbm, gain2_hbm, shift2_hbm, bias_hbm)
    lane_load = [pltpu.make_async_copy(v, lanes.at[i], load_sem.at[3 + i]) for i, v in enumerate(lane_hbm)]
    gain1, shift1, gain2, shift2, bias = [lanes.at[i] for i in range(5)]
    for load in (*w_load, *lane_load):
        load.start()

    barrier = pltpu.get_barrier_semaphore()

    def ring(at, step, count):
        return jnp.where(at + step >= count, at + step - count, at + step)

    def for_others(body):
        if n_all <= 32:
            for steps in itertools.product(range(n_tm), range(n_row), range(n_col)):
                if any(steps):
                    body(tuple(ring(*each) for each in zip((tm, row, col), steps, counts)))
        else:
            lax.fori_loop(1, n_all, lambda i, _: (body(place(lax.rem(rank + i, n_all))), 0)[1], 0)

    def greet(other):
        pl.semaphore_signal(barrier, inc=1, device_id=other, device_id_type=MESH)

    for_others(greet)

    def halo_copy(layer, source, k):
        ahead, down, right = STEPS[k]
        if right == 0:
            side = (1 - down) // 2
            src = source.at[:, height - 1 if down == 1 else 0]
            dst = got_rows.at[layer, ahead, side]
        elif down == 0:
            side = (1 - right) // 2
            src = edge_cols.at[layer, side]
            dst = got_cols.at[layer, ahead, side]
        else:
            r_side, c_side = (1 - down) // 2, (1 - right) // 2
            src = corners.at[layer, r_side, c_side]
            dst = got_corners.at[layer, ahead, r_side, c_side]
        return pltpu.make_async_remote_copy(
            src_ref=src,
            dst_ref=dst,
            send_sem=halo_send.at[layer, k],
            recv_sem=halo_recv.at[layer, k],
            device_id=(tm + ahead, row + down, col + right),
            device_id_type=MESH,
        )

    def front_copy(layer, source, frame):
        return pltpu.make_async_remote_copy(
            src_ref=source.at[frame],
            dst_ref=front.at[layer, frame],
            send_sem=front_send.at[layer, frame],
            recv_sem=front_recv.at[layer, frame],
            device_id=(tm + 1, row, col),
            device_id_type=MESH,
        )

    def send_front(layer, source, frame):
        @pl.when(tm + 1 < n_tm)
        def _():
            front_copy(layer, source, frame).start()

    def for_sends(layer, source, act):
        for k, step in enumerate(STEPS):

            @pl.when(exists(*step))
            def _():
                act(halo_copy(layer, source, k))

    def wait_halo(layer, source, ahead):
        for k, step in enumerate(STEPS):
            if step[0] == ahead:

                @pl.when(exists(-step[0], -step[1], -step[2]))
                def _():
                    halo_copy(layer, source, k).wait_recv()

    def pack_edges(layer, source):
        for r_side in range(2):
            for c_side in range(2):
                corners[layer, r_side, c_side] = jnp.zeros((8, channels), F32)
        for frame in range(frames):
            for c_side, w in ((0, width - 1), (1, 0)):
                for h in range(height):
                    line = source[frame, h, w : w + 1, :]
                    edge_cols[layer, c_side, frame, h : h + 1, :] = line
                    if h in (0, height - 1):
                        corners[layer, 0 if h else 1, c_side, frame : frame + 1, :] = line

    def stat_copy(layer, other):
        return pltpu.make_async_remote_copy(
            src_ref=stats.at[layer, rank],
            dst_ref=stats.at[layer, rank],
            send_sem=stat_send.at[layer],
            recv_sem=stat_recv.at[layer],
            device_id=other,
            device_id_type=MESH,
        )

    def stat_wait(layer):
        others = stats.at[layer, pl.ds(0, n_all - 1)]
        return pltpu.make_async_remote_copy(
            src_ref=others,
            dst_ref=others,
            send_sem=stat_send.at[layer],
            recv_sem=stat_recv.at[layer],
            device_id=place(lax.rem(rank + 1, n_all)),
            device_id_type=MESH,
        )

    def local_stats(layer, source):
        values = source[...].reshape(cells, channels)
        mean = jnp.sum(values, axis=0, keepdims=True) * (1.0 / cells)
        centered = values - mean
        stats[layer, rank, 0:1] = mean
        stats[layer, rank, 1:2] = jnp.sum(centered * centered, axis=0, keepdims=True)

    def joined(layer):
        block = stats[layer]
        total = jnp.sum(block, axis=0)
        center = jnp.broadcast_to(total[0:1], (8, channels))
        center = group_total(center)[0:1] * (1.0 / (n_all * per_group))
        away = block[:, 0:1, :] - center[None]
        spread = total[1:2] + float(cells) * jnp.sum(away * away, axis=0)
        spread = group_total(jnp.broadcast_to(spread, (8, channels)))[0:1]
        return center, spread * (1.0 / (float(cells) * n_all * per_group))

    def convert(layer):
        w_load[layer].wait()
        piece = channels

        def body(i, _):
            at = pl.ds(pl.multiple_of(i * piece, piece), piece)
            for dt in range(3):
                w_high, w_low = split(w_raw[layer, dt, at, :])
                w_split[layer, dt, at, 0:channels] = w_high
                w_split[layer, dt, at, channels:] = w_low
            return 0

        lax.fori_loop(0, 9, body, 0)

    column = lax.broadcasted_iota(jnp.int32, (height, width, channels), 1)

    def store_taps(frame, first, value, left, right):
        rows = value.shape[0]
        at = column[:rows]
        before = jnp.where(at == 0, left[:, None, :], pltpu.roll(value, 1, 1))
        after = jnp.where(at == width - 1, right[:, None, :], pltpu.roll(value, width - 1, 1))
        for j, shifted in enumerate((before, value, after)):
            v_high, v_low = split(shifted)
            high[frame, first : first + rows, :, j * channels : (j + 1) * channels] = v_high
            low[frame, first : first + rows, :, j * channels : (j + 1) * channels] = v_low

    def spread_frame(layer, source, ahead, frame, activate):
        to = frame + frames * (1 - ahead)

        def valid(down, right, value):
            return jnp.where(exists(-ahead, -down, -right), value, 0.0)

        left = valid(0, 1, activate(got_cols[layer, ahead, 0, frame]))
        right = valid(0, -1, activate(got_cols[layer, ahead, 1, frame]))
        store_taps(to, 1, activate(source[frame]), left, right)
        for side, down in ((0, 1), (1, -1)):
            line = valid(down, 0, activate(got_rows[layer, ahead, side, frame]))
            left = valid(down, 1, activate(got_corners[layer, ahead, side, 0, frame : frame + 1]))
            right = valid(down, -1, activate(got_corners[layer, ahead, side, 1, frame : frame + 1]))
            store_taps(to, 0 if side == 0 else height + 1, line[None], left, right)

    def lines(array, frame):
        return jnp.concatenate(
            [array[frame, dh : dh + height].reshape(height * width, 3 * channels) for dh in range(3)], axis=1
        )

    def dot(a, b):
        return jnp.dot(a, b, preferred_element_type=F32)

    def fold(value):
        return value[:, :channels] + value[:, channels:]

    def conv_pair(layer, frame, near):
        w = [w_split.at[layer, dt] for dt in range(3)]
        first, second = (2, 1) if near else (1, 0)
        h, l = lines(high, frame), lines(low, frame)
        both = dot(l, jnp.concatenate([w[first][:, :channels], w[second][:, :channels]], axis=1))
        out_second = fold(dot(h, w[second][...])) + both[:, channels:]
        return fold(dot(h, w[first][...])) + both[:, :channels], out_second

    def conv_own(layer):
        w = [w_split.at[layer, dt] for dt in range(3)]
        size = height * width
        first = lines(high, 2)
        shared = fold(dot(jnp.concatenate([first, lines(high, 3)], axis=0), w[2][...]))
        lows = jnp.concatenate([lines(low, 2), lines(low, 3)], axis=0)
        both = dot(lows, jnp.concatenate([w[2][:, :channels], w[1][:, :channels]], axis=1))
        out_second = shared[size:] + fold(dot(first, w[1][...])) + both[:size, channels:] + both[size:, :channels]
        return shared[:size] + both[:size, :channels], out_second

    def conv_one(layer, frame, dt):
        w = w_split.at[layer, dt]
        return fold(dot(lines(high, frame), w[...])) + dot(lines(low, frame), w[:, :channels])

    def start_stats(layer):
        for_others(lambda other: stat_copy(layer, other).start())

    def layer_pass(layer, source, gain, shift, beside, emit):
        if layer == 0:
            convert(0)
        stat_wait(layer).wait_recv()
        center, spread = joined(layer)
        scale = lax.rsqrt(spread + epsilon)

        def activate(value):
            lead = (1,) * (value.ndim - 2) + (1, channels)
            u = (value - center.reshape(lead)) * scale.reshape(lead) * gain[...].reshape(lead)
            u = u + shift[...].reshape(lead)
            return u / (1.0 + jnp.exp(-u))

        wait_halo(layer, source, 0)
        for frame in range(frames):
            spread_frame(layer, source, 0, frame, activate)
        part[0], part[1] = conv_own(layer)
        beside()
        wait_halo(layer, source, 1)

        def arrived(frame):
            @pl.when(tm == 0)
            def _():
                high[frame] = high[2]
                low[frame] = low[2]

            @pl.when(tm != 0)
            def _():
                front_copy(layer, source, frame).wait_recv()
                spread_frame(layer, front.at[layer], 1, frame, activate)

        arrived(1)
        first, second = conv_pair(layer, 1, False)
        part[0] += first
        emit(1, part[1] + second)
        arrived(0)
        emit(0, part[0] + conv_one(layer, 0, 0))

    def keep_hidden(frame, value):
        hid_ref[frame] = value.reshape(height, width, channels)
        if frame == 1:
            send_front(1, hid_ref, 1)

    def keep_output(frame, value):
        moved = value.reshape(height, width, channels)
        out_ref[frame] = x_ref[frame] + moved + bias[...].reshape(1, 1, channels)

    feat_load.wait()
    for load in lane_load:
        load.wait()
    local_stats(0, x_ref)
    pack_edges(0, x_ref)
    pl.semaphore_wait(barrier, n_all - 1)
    start_stats(0)
    send_front(0, x_ref, 1)
    for_sends(0, x_ref, lambda c: c.start())
    send_front(0, x_ref, 0)
    layer_pass(0, x_ref, gain1, shift1, lambda: convert(1), keep_hidden)
    local_stats(1, hid_ref)
    start_stats(1)
    pack_edges(1, hid_ref)
    for_sends(1, hid_ref, lambda c: c.start())
    send_front(1, hid_ref, 0)
    layer_pass(1, hid_ref, gain2, shift2, lambda: None, keep_output)

    for layer, source in enumerate((x_ref, hid_ref)):
        stat_wait(layer).wait_send()
        for_sends(layer, source, lambda c: c.wait_send())

        @pl.when(tm + 1 < n_tm)
        def _():
            for frame in range(frames):
                front_copy(layer, source, frame).wait_send()


def local(counts, features, gain1, shift1, weight1, gain2, shift2, weight2, bias):
    n_tm, n_row, n_col = counts
    frames, height, width, channels = features.shape
    taps = 9 * channels
    lane = lambda v: v.reshape(1, channels)
    weights = lambda w: w.reshape(3, taps, channels)
    vmem = pl.BlockSpec(memory_space=pltpu.VMEM)
    hbm = pl.BlockSpec(memory_space=pltpu.HBM)
    padded = (2 * frames, height + 2, width, 3 * channels)
    dma = pltpu.SemaphoreType.DMA
    return pl.pallas_call(
        functools.partial(kernel, counts),
        out_shape=jax.ShapeDtypeStruct(features.shape, F32),
        in_specs=[hbm] * 8,
        out_specs=vmem,
        scratch_shapes=[
            pltpu.VMEM((5, 1, channels), F32),
            pltpu.VMEM(features.shape, F32),
            pltpu.VMEM(features.shape, F32),
            pltpu.VMEM((2, 3, taps, channels), F32),
            pltpu.VMEM((2, 3, taps, 2 * channels), BF16),
            pltpu.VMEM(padded, BF16),
            pltpu.VMEM(padded, BF16),
            pltpu.VMEM((2, height * width, channels), F32),
            pltpu.VMEM((2, 2, frames, height, channels), F32),
            pltpu.VMEM((2, 2, 2, 8, channels), F32),
            pltpu.VMEM((2, *features.shape), F32),
            pltpu.VMEM((2, 2, 2, frames, width, channels), F32),
            pltpu.VMEM((2, 2, 2, frames, height, channels), F32),
            pltpu.VMEM((2, 2, 2, 2, 8, channels), F32),
            pltpu.VMEM((2, n_tm * n_row * n_col, 2, channels), F32),
            dma((8,)),
            dma((2, len(STEPS))),
            dma((2, len(STEPS))),
            dma((2, frames)),
            dma((2, frames)),
            dma((2,)),
            dma((2,)),
        ],
        compiler_params=pltpu.CompilerParams(
            collective_id=0, has_side_effects=True, vmem_limit_bytes=60 * 1024 * 1024
        ),
    )(features, lane(gain1), lane(shift1), weights(weight1), lane(gain2), lane(shift2), weights(weight2), lane(bias))


def solution(mesh):
    counts = tuple(mesh.shape[axis] for axis in ("tm", "row", "col"))
    in_specs = (P("tm", "row", "col", None), P(), P(), P(), P(), P(), P(), P())
    out_specs = P("tm", "row", "col", None)
    return jax.shard_map(
        functools.partial(local, counts), mesh=mesh, in_specs=in_specs, out_specs=out_specs, check_vma=False
    )
```
